32 devices in a mesh: island: 4 (over y, x), fsdp: 8 (over z, core).
Axes of the slice: x: 2, y: 2, z: 4, core: 2. Of those that a mesh axis runs over, the one named last changes fastest.
Arguments:
- pseudo_grad: bfloat16 [4, 14336, 4096], P('island', 'fsdp'), may hold values from -110 to 110
- error_buffer: bfloat16 [4, 14336, 4096], P('island', 'fsdp'), may hold values from -3 to 3
- basis_init: float32 [4096, 64], replicated, may hold values from -6 to 6
- params: float32 [14336, 4096], P(('fsdp', 'island')), may hold values from -6 to 6
- momentum: float32 [14336, 4096], P(('fsdp', 'island')), may hold values from -6 to 6
Outputs:
- new_error: bfloat16 [4, 14336, 4096], P('island', 'fsdp')
- new_params: float32 [14336, 4096], P(('fsdp', 'island'))
- new_momentum: float32 [14336, 4096], P(('fsdp', 'island'))
The draws below stay inside these ranges and needn't reach their ends.
All inputs are finite; a program needn't handle non-finite values.
Results may differ from the reference program's by a relative error of at most 0.0051.
Values sent between devices are 32-bit elements; how exact they have to be, the bound alone decides.
A program may use at most 192 MiB of HBM per device.

```python
import math
import jax
import jax.numpy as jnp
from jax import lax

D = 4096
FF = 14336
R = 64
ITERS = 4
ISLANDS = 4


def draw_pseudo_grad(key, part):
    subkeys = jax.random.split(key, 3)
    position = jnp.arange(FF, dtype=jnp.float32) / FF
    row_scale = jnp.exp(math.log(3.0) * position + math.log(4.0) * jax.random.uniform(subkeys[1], (FF,), jnp.float32))
    column_scale = jnp.exp(math.log(3.0) * jax.random.uniform(subkeys[2], (D,), jnp.float32))
    island_scale = jnp.exp(math.log(3.0) * jnp.arange(ISLANDS, dtype=jnp.float32) / max(ISLANDS - 1, 1))
    fluctuation = jnp.clip(jax.random.normal(subkeys[0], (ISLANDS, FF, D), jnp.float32), -4.0, 4.0)
    result = 0.1 * fluctuation * row_scale[None, :, None] * column_scale[None, None, :] * island_scale[:, None, None]
    return result.astype(jnp.bfloat16)


def level_of(key, extent, cuts, smallest, high):
    level = 1.0
    for dim, blocks in cuts:
        steps = jax.random.uniform(jax.random.fold_in(jax.random.fold_in(key, 6), dim), (blocks,), jnp.float32, smallest / len(cuts), high / len(cuts))
        level = level * jnp.repeat(jnp.exp(steps), extent[dim] // blocks).reshape((-1,) + (1,) * (len(extent) - 1 - dim))
    return level


def noise(own_key, extent, deviation, reach, pieces=(), kind=jnp.bfloat16):
    gain = level_of(own_key, extent, pieces, -0.22, 0.18) if pieces else 1.0
    values = jax.random.normal(own_key, extent, jnp.float32) * deviation * gain
    return jnp.minimum(jnp.maximum(values, -reach), reach).astype(kind)


def setup_inputs(seed: int = 0) -> dict:
    splits = jax.random.split(jax.random.key(seed), 6)
    pseudo_grad = draw_pseudo_grad(jax.random.fold_in(splits[5], 71), 0)
    error_buffer = noise(splits[1], (ISLANDS, FF, D), 0.5, 3.0, ((0, 4), (1, 8)))
    basis_init = noise(splits[2], (D, R), 1.0, 6.0, (), jnp.float32)
    params = noise(splits[3], (FF, D), 1.0, 6.0, ((0, 32),), jnp.float32)
    momentum = noise(splits[4], (FF, D), 1.0, 6.0, ((0, 32),), jnp.float32)
    return dict(pseudo_grad=pseudo_grad, error_buffer=error_buffer, basis_init=basis_init, params=params, momentum=momentum)


momentum_coef = 0.9
outer_rate = 0.7

def reference(pseudo_grad, error_buffer, basis_init, params, momentum):
    combined = (pseudo_grad.astype(jnp.float32) + error_buffer.astype(jnp.float32)).astype(jnp.bfloat16)
    wide = combined.astype(jnp.float32)
    summed = jnp.sum(wide, axis=0)
    right_basis = basis_init
    for sweep in range(ITERS):
        sketch = jnp.dot(summed.astype(jnp.float32), right_basis.astype(jnp.float32), precision=lax.Precision.HIGHEST, preferred_element_type=jnp.float32)
        gram = jnp.dot(sketch.T.astype(jnp.float32), sketch.astype(jnp.float32), precision=lax.Precision.HIGHEST, preferred_element_type=jnp.float32)
        factor = jnp.linalg.cholesky(gram)
        orthonormal = lax.linalg.triangular_solve(factor, sketch, left_side=False, lower=True, transpose_a=True)
        right_basis = jnp.dot(summed.T.astype(jnp.float32), orthonormal.astype(jnp.float32), precision=lax.Precision.HIGHEST, preferred_element_type=jnp.float32)
    approx = jnp.dot(orthonormal.astype(jnp.float32), right_basis.T.astype(jnp.float32), precision=lax.Precision.HIGHEST, preferred_element_type=jnp.float32) * (1.0 / ISLANDS)
    new_error = (wide - approx[None]).astype(jnp.bfloat16)
    new_momentum = momentum_coef * momentum + approx
    new_params = params - outer_rate * (approx + momentum_coef * new_momentum)
    return (new_error, new_params, new_momentum)
```

```python
import functools

import jax
import jax.numpy as jnp
from jax import lax
from jax.experimental import pallas as pl
from jax.experimental.pallas import tpu as pltpu
from jax.sharding import PartitionSpec as P

ITERS = 4

momentum_coef = 0.9
outer_rate = 0.7

MESH = pl.DeviceIdType.MESH
F32 = jnp.float32
BF16 = jnp.bfloat16
HIGH = lax.Precision.HIGHEST


def split(value):
    high = value.astype(BF16)
    low = (value - high.astype(F32)).astype(BF16)
    return high, low


def bits_of(extent):
    return extent.bit_length() - 1


def tile_of(extent, want):
    return want if extent % want == 0 else extent


def partner_of(index, bit):
    stride = 1 << bit
    own = (index // stride) % 2
    return index + (1 - 2 * own) * stride, own


def power_kernel(
    islands,
    shards,
    grad_ref,
    error_ref,
    basis_ref,
    combined_out,
    left_out,
    right_out,
    combined,
    grad_stage,
    error_stage,
    basis_parts,
    sketch,
    sketch_in,
    sketch_parts,
    gram,
    gram_in,
    work,
    projected,
    core_in,
    held,
    first_in,
    first,
    second_in,
    second,
    line_in,
    first_all,
    held_all,
    projected_all,
    stage_sem,
    out_sem,
    send_sem,
    recv_sem,
):
    island = lax.axis_index("island")
    shard = lax.axis_index("fsdp")
    rows, wide = combined.shape
    rank = sketch.shape[0]
    half_rank, half_wide = rank // 2, wide // 2
    island_bits, shard_bits = bits_of(islands), bits_of(shards)

    def island_peer(bit):
        index, own = partner_of(island, bit)
        return (index, shard), own

    def shard_peer(bit):
        index, own = partner_of(shard, bit)
        return (island, index), own

    peers = [island_peer(b)[0] for b in range(island_bits)] + [shard_peer(b)[0] for b in range(shard_bits)]

    counter = [0]

    def send(src, dst, peer):
        number = counter[0]
        counter[0] += 1
        copy = pltpu.make_async_remote_copy(
            src_ref=src,
            dst_ref=dst,
            send_sem=send_sem.at[number],
            recv_sem=recv_sem.at[number],
            device_id=peer,
            device_id_type=MESH,
        )
        copy.start()
        return copy

    tile = tile_of(rows, 256)
    tiles = rows // tile

    def fetch(t, slot):
        span = pl.ds(pl.multiple_of(t * tile, tile), tile)
        return (
            pltpu.make_async_copy(grad_ref.at[0, span], grad_stage.at[slot], stage_sem.at[0, slot]),
            pltpu.make_async_copy(error_ref.at[0, span], error_stage.at[slot], stage_sem.at[1, slot]),
        )

    for copy in fetch(0, 0):
        copy.start()

    barrier = pltpu.get_barrier_semaphore()
    for peer in peers:
        pl.semaphore_signal(barrier, inc=1, device_id=peer, device_id_type=MESH)
    pl.semaphore_wait(barrier, len(peers))

    strip = tile_of(wide, 512)
    strips = wide // strip

    def strip_span(s):
        return pl.ds(pl.multiple_of(s * strip, strip), strip)

    @pl.loop(0, strips)
    def _(s):
        span = strip_span(s)
        high, low = split(basis_ref[:, span])
        basis_parts[0:rank, span] = high
        basis_parts[rank:, span] = low

    def sketch_tile(t):
        span = pl.ds(pl.multiple_of(t * tile, tile), tile)
        both = lax.dot_general(
            basis_parts[...], combined[span, :], (((1,), (1,)), ((), ())), preferred_element_type=F32
        )
        sketch[:, span] = both[0:rank] + both[rank:]

    @pl.loop(0, tiles)
    def _(t):
        slot = lax.rem(t, 2)

        @pl.when(t + 1 < tiles)
        def _():
            for copy in fetch(t + 1, 1 - slot):
                copy.start()

        for copy in fetch(t, slot):
            copy.wait()

        @pl.loop(0, tile // 16)
        def _(r):
            part = pl.ds(pl.multiple_of(r * 16, 16), 16)
            total = grad_stage[slot, part, :].astype(F32) + error_stage[slot, part, :].astype(F32)
            combined[pl.ds(pl.multiple_of(t * tile + r * 16, 16), 16), :] = total.astype(BF16)

        sketch_tile(t)

    keep = pltpu.make_async_copy(combined, combined_out, out_sem)
    keep.start()

    lane = lax.broadcasted_iota(jnp.int32, (rank, 2 * rank), 1)
    line = lax.broadcasted_iota(jnp.int32, (rank, 2 * rank), 0)

    def eliminate(begin, end):
        def step(j, carry):
            value = work[...]
            row = work[pl.ds(j, 1), :]
            column = jnp.sum(jnp.where(lane == j + rank, value, 0.0), axis=1, keepdims=True)
            pivot = jnp.sum(jnp.where(lane[0:1] == j + rank, row, 0.0), axis=1, keepdims=True)
            scale = jnp.where(line[:, 0:1] > j, column / pivot, 0.0)
            work[...] = value - scale * row
            return carry

        lax.fori_loop(begin, end, step, 0)

    stages = 2 + 2 * 2 + (shard_bits - 1)

    def iteration(sweep, carry):
        counter[0] = 0
        for s in range(island_bits):
            one = send(
                sketch.at[0:half_rank], sketch_in.at[s, 0:half_rank], island_peer(s)[0]
            )
            two = send(
                sketch.at[half_rank:rank], sketch_in.at[s, half_rank:rank], island_peer(island_bits - 1 - s)[0]
            )
            one.wait()
            two.wait()
            sketch[...] += sketch_in[s]
        high, low = split(sketch[...])
        sketch_parts[0:rank] = high
        sketch_parts[rank:] = low

        value = sketch[...]
        gram[...] = lax.dot_general(
            value,
            jnp.concatenate([value, value], axis=0),
            (((1,), (1,)), ((), ())),
            precision=HIGH,
            preferred_element_type=F32,
        )

        def project(begin, end):
            @pl.loop(begin, end)
            def _(s):
                span = strip_span(s)
                both = jnp.dot(sketch_parts[...], combined[:, span], preferred_element_type=F32)
                projected[:, span] = both[0:rank] + both[rank:]

        cuts = [strips * i // shard_bits for i in range(shard_bits + 1)]
        for s in range(shard_bits):
            copy = send(gram, gram_in.at[s], shard_peer(s)[0])
            project(cuts[s], cuts[s + 1])
            copy.wait()
            gram[...] += gram_in[s]
        work[...] = jnp.where(lane < rank, jnp.where(lane == line, 1.0, 0.0), gram[...])

        place = [0]

        def finish(*copies):
            begin = rank * place[0] // stages
            place[0] += 1
            eliminate(begin, rank * place[0] // stages)
            for copy in copies:
                copy.wait()

        core_peer, core = shard_peer(0)
        own = pl.ds(pl.multiple_of(core * half_rank, half_rank), half_rank)
        other = pl.ds(pl.multiple_of((1 - core) * half_rank, half_rank), half_rank)
        finish(send(projected.at[other], core_in, core_peer))
        held[...] = projected[own, :] + core_in[...]

        left, right = slice(0, half_wide), slice(half_wide, wide)
        peer_a, bit_a = island_peer(0)
        peer_b, bit_b = island_peer(1)
        quarter, eighth = half_rank // 2, half_rank // 4

        def part(index, size):
            return pl.ds(pl.multiple_of(index * size, size), size)

        finish(
            send(held.at[part(1 - bit_a, quarter), left], first_in.at[:, left], peer_a),
            send(held.at[part(1 - bit_b, quarter), right], first_in.at[:, right], peer_b),
        )
        first[:, left] = held[part(bit_a, quarter), left] + first_in[:, left]
        first[:, right] = held[part(bit_b, quarter), right] + first_in[:, right]
        finish(
            send(first.at[part(1 - bit_b, eighth), left], second_in.at[:, left], peer_b),
            send(first.at[part(1 - bit_a, eighth), right], second_in.at[:, right], peer_a),
        )
        second[:, left] = first[part(bit_b, eighth), left] + second_in[:, left]
        second[:, right] = first[part(bit_a, eighth), right] + second_in[:, right]
        for s in range(1, shard_bits):
            finish(send(second, line_in.at[s - 1], shard_peer(s)[0]))
            second[...] += line_in[s - 1]

        first_all[part(bit_b, eighth), left] = second[:, left]
        first_all[part(bit_a, eighth), right] = second[:, right]
        finish(
            send(second.at[:, left], first_all.at[part(bit_b, eighth), left], peer_b),
            send(second.at[:, right], first_all.at[part(bit_a, eighth), right], peer_a),
        )
        held_all[part(bit_a, quarter), left] = first_all[:, left]
        held_all[part(bit_b, quarter), right] = first_all[:, right]
        finish(
            send(first_all.at[:, left], held_all.at[part(bit_a, quarter), left], peer_a),
            send(first_all.at[:, right], held_all.at[part(bit_b, quarter), right], peer_b),
        )
        projected_all[own, :] = held_all[...]
        finish(send(held_all, projected_all.at[own], core_peer))

        value = work[...]
        diagonal = jnp.sum(jnp.where(lane == line + rank, value, 0.0), axis=1, keepdims=True)
        inverse = (value * (1.0 / jnp.sqrt(diagonal)))[:, 0:rank]

        @pl.when(sweep < ITERS - 1)
        def _():
            @pl.loop(0, strips)
            def _(s):
                span = strip_span(s)
                basis = jnp.dot(inverse, projected_all[:, span], precision=HIGH, preferred_element_type=F32)
                high, low = split(basis)
                basis_parts[0:rank, span] = high
                basis_parts[rank:, span] = low

            @pl.loop(0, tiles)
            def _(t):
                sketch_tile(t)

        @pl.when(sweep == ITERS - 1)
        def _():
            @pl.loop(0, strips)
            def _(s):
                span = strip_span(s)
                basis = jnp.dot(inverse, projected_all[:, span], precision=HIGH, preferred_element_type=F32)
                high, low = split(basis * (1.0 / islands))
                right_out[0:rank, span] = high
                right_out[rank : 2 * rank, span] = low
                right_out[2 * rank :, span] = high

            orthonormal = jnp.dot(inverse, sketch[...], precision=HIGH, preferred_element_type=F32)
            high, low = split(orthonormal)
            left_out[0:rank, :] = high
            left_out[rank : 2 * rank, :] = high
            left_out[2 * rank :, :] = low

        return carry

    lax.fori_loop(0, ITERS, iteration, 0)
    keep.wait()


def outer_kernel(combined_ref, left_ref, own_left_ref, right_ref, params_ref, momentum_ref, error_out, params_out, momentum_out):
    approx = jnp.dot(left_ref[...], right_ref[...], preferred_element_type=F32)
    error_out[0] = (combined_ref[...].astype(F32) - approx).astype(BF16)
    own = jnp.dot(own_left_ref[0], right_ref[...], preferred_element_type=F32)
    new_momentum = momentum_coef * momentum_ref[...] + own
    momentum_out[...] = new_momentum
    params_out[...] = params_ref[...] - outer_rate * (own + momentum_coef * new_momentum)


def steps_of(rows, quarter):
    for steps in (28, 14, 7, 4, 2):
        if rows % (16 * steps) == 0 and quarter % (8 * steps) == 0:
            return steps
    return 1


def shards(islands, shard_count, pseudo_grad, error_buffer, basis_init, params, momentum):
    _, rows, wide = pseudo_grad.shape
    rank = basis_init.shape[1]
    quarter = params.shape[0]
    half, tile = rank // 2, tile_of(rows, 256)
    island_bits, shard_bits = bits_of(islands), bits_of(shard_count)
    sends = 2 * island_bits + shard_bits + 2 + 2 * 4 + (shard_bits - 1)
    vmem = pl.BlockSpec(memory_space=pltpu.VMEM)
    hbm = pl.BlockSpec(memory_space=pl.ANY)
    combined, left, right = pl.pallas_call(
        functools.partial(power_kernel, islands, shard_count),
        out_shape=(
            jax.ShapeDtypeStruct((rows, wide), BF16),
            jax.ShapeDtypeStruct((3 * rank, rows), BF16),
            jax.ShapeDtypeStruct((3 * rank, wide), BF16),
        ),
        in_specs=[hbm, hbm, vmem],
        out_specs=(hbm, vmem, vmem),
        scratch_shapes=[
            pltpu.VMEM((rows, wide), BF16),
            pltpu.VMEM((2, tile, wide), BF16),
            pltpu.VMEM((2, tile, wide), BF16),
            pltpu.VMEM((2 * rank, wide), BF16),
            pltpu.VMEM((rank, rows), F32),
            pltpu.VMEM((island_bits, rank, rows), F32),
            pltpu.VMEM((2 * rank, rows), BF16),
            pltpu.VMEM((rank, 2 * rank), F32),
            pltpu.VMEM((shard_bits, rank, 2 * rank), F32),
            pltpu.VMEM((rank, 2 * rank), F32),
            pltpu.VMEM((rank, wide), F32),
            pltpu.VMEM((half, wide), F32),
            pltpu.VMEM((half, wide), F32),
            pltpu.VMEM((half // 2, wide), F32),
            pltpu.VMEM((half // 2, wide), F32),
            pltpu.VMEM((half // 4, wide), F32),
            pltpu.VMEM((half // 4, wide), F32),
            pltpu.VMEM((max(shard_bits - 1, 1), half // 4, wide), F32),
            pltpu.VMEM((half // 2, wide), F32),
            pltpu.VMEM((half, wide), F32),
            pltpu.VMEM((rank, wide), F32),
            pltpu.SemaphoreType.DMA((2, 2)),
            pltpu.SemaphoreType.DMA,
            pltpu.SemaphoreType.DMA((sends,)),
            pltpu.SemaphoreType.DMA((sends,)),
        ],
        compiler_params=pltpu.CompilerParams(
            collective_id=0, has_side_effects=True, vmem_limit_bytes=56 * 1024 * 1024
        ),
        name="power_iterations",
    )(pseudo_grad, error_buffer, basis_init.T)

    left = left.T
    steps = steps_of(rows, quarter)
    own_left = lax.dynamic_slice_in_dim(left, lax.axis_index("island") * quarter, quarter, 0)
    own_left = own_left.reshape(steps, quarter // steps, 3 * rank)
    tall, short = rows // steps, quarter // steps
    new_error, new_params, new_momentum = pl.pallas_call(
        outer_kernel,
        grid=(steps,),
        out_shape=(
            jax.ShapeDtypeStruct((1, rows, wide), BF16),
            jax.ShapeDtypeStruct((quarter, wide), F32),
            jax.ShapeDtypeStruct((quarter, wide), F32),
        ),
        in_specs=[
            pl.BlockSpec((tall, wide), lambda i: (i, 0)),
            pl.BlockSpec((tall, 3 * rank), lambda i: (i, 0)),
            pl.BlockSpec((1, short, 3 * rank), lambda i: (i, 0, 0)),
            pl.BlockSpec((3 * rank, wide), lambda i: (0, 0)),
            pl.BlockSpec((short, wide), lambda i: (i, 0)),
            pl.BlockSpec((short, wide), lambda i: (i, 0)),
        ],
        out_specs=(
            pl.BlockSpec((1, tall, wide), lambda i: (0, i, 0)),
            pl.BlockSpec((short, wide), lambda i: (i, 0)),
            pl.BlockSpec((short, wide), lambda i: (i, 0)),
        ),
        compiler_params=pltpu.CompilerParams(vmem_limit_bytes=48 * 1024 * 1024),
        name="outer_step",
    )(combined, left, own_left, right, params, momentum)
    return (new_error, new_params, new_momentum)


def solution(mesh):
    placed = (
        P("island", "fsdp", None),
        P("island", "fsdp", None),
        P(),
        P(("fsdp", "island"), None),
        P(("fsdp", "island"), None),
    )
    return jax.shard_map(
        functools.partial(shards, mesh.shape["island"], mesh.shape["fsdp"]),
        mesh=mesh,
        in_specs=placed,
        out_specs=(
            P("island", "fsdp", None),
            P(("fsdp", "island"), None),
            P(("fsdp", "island"), None),
        ),
        check_vma=False,
    )
```

```python
import functools

import jax
import jax.numpy as jnp
from jax import lax
from jax.experimental import pallas as pl
from jax.experimental.pallas import tpu as pltpu
from jax.sharding import PartitionSpec as P

ITERS = 4

momentum_coef = 0.9
outer_rate = 0.7

MESH = pl.DeviceIdType.MESH
F32 = jnp.float32
BF16 = jnp.bfloat16
HIGH = lax.Precision.HIGHEST


def split(value):
    high = value.astype(BF16)
    low = (value - high.astype(F32)).astype(BF16)
    return high, low


def bits_of(extent):
    return extent.bit_length() - 1


def tile_of(extent, want):
    return want if extent % want == 0 else extent


def partner_of(index, bit):
    stride = 1 << bit
    own = (index // stride) % 2
    return index + (1 - 2 * own) * stride, own


def power_kernel(
    islands,
    shards,
    grad_ref,
    error_ref,
    basis_ref,
    combined_out,
    left_out,
    right_out,
    combined,
    grad_stage,
    error_stage,
    basis_parts,
    sketch,
    sketch_in,
    sketch_parts,
    gram,
    gram_in,
    work,
    projected,
    core_in,
    held,
    first_in,
    first,
    second_in,
    second,
    line_in,
    second_all,
    first_all,
    held_all,
    projected_all,
    stage_sem,
    out_sem,
    send_sem,
    recv_sem,
):
    island = lax.axis_index("island")
    shard = lax.axis_index("fsdp")
    rows, wide = combined.shape
    rank = sketch.shape[0]
    half_rank = rank // 2
    island_bits, shard_bits = bits_of(islands), bits_of(shards)

    def island_peer(bit):
        index, own = partner_of(island, bit)
        return (index, shard), own

    def shard_peer(bit):
        index, own = partner_of(shard, bit)
        return (island, index), own

    peers = [island_peer(b)[0] for b in range(island_bits)] + [shard_peer(b)[0] for b in range(shard_bits)]

    counter = [0]

    def send(src, dst, peer):
        number = counter[0]
        counter[0] += 1
        copy = pltpu.make_async_remote_copy(
            src_ref=src,
            dst_ref=dst,
            send_sem=send_sem.at[number],
            recv_sem=recv_sem.at[number],
            device_id=peer,
            device_id_type=MESH,
        )
        copy.start()
        return copy

    tile = tile_of(rows, 256)
    tiles = rows // tile

    def fetch(t, slot):
        span = pl.ds(pl.multiple_of(t * tile, tile), tile)
        return (
            pltpu.make_async_copy(grad_ref.at[0, span], grad_stage.at[slot], stage_sem.at[0, slot]),
            pltpu.make_async_copy(error_ref.at[0, span], error_stage.at[slot], stage_sem.at[1, slot]),
        )

    for copy in fetch(0, 0):
        copy.start()

    barrier = pltpu.get_barrier_semaphore()
    for peer in peers:
        pl.semaphore_signal(barrier, inc=1, device_id=peer, device_id_type=MESH)
    pl.semaphore_wait(barrier, len(peers))

    strip = tile_of(wide, 512)
    strips = wide // strip

    def strip_span(s):
        return pl.ds(pl.multiple_of(s * strip, strip), strip)

    @pl.loop(0, strips)
    def _(s):
        span = strip_span(s)
        high, low = split(basis_ref[:, span])
        basis_parts[0:rank, span] = high
        basis_parts[rank:, span] = low

    cut = (tiles + 1) // 2
    row_chunks = [(0, cut), (cut, tiles)] if tiles > 1 else [(0, 1)]
    row_spans = [slice(begin * tile, end * tile) for begin, end in row_chunks]
    chunk_strips = [(c * strips // 2, (c + 1) * strips // 2) for c in range(2)]
    columns = [slice(begin * strip, end * strip) for begin, end in chunk_strips]

    def tile_span(t):
        return pl.ds(pl.multiple_of(t * tile, tile), tile)

    def sketch_part(t, cols):
        both = lax.dot_general(
            basis_parts[:, cols],
            combined[tile_span(t), cols],
            (((1,), (1,)), ((), ())),
            preferred_element_type=F32,
        )
        return both[0:rank] + both[rank:]

    def stream(begin, end):
        @pl.loop(begin, end)
        def _(t):
            slot = lax.rem(t, 2)

            @pl.when(t + 1 < tiles)
            def _():
                for copy in fetch(t + 1, 1 - slot):
                    copy.start()

            for copy in fetch(t, slot):
                copy.wait()

            @pl.loop(0, tile // 16)
            def _(r):
                part = pl.ds(pl.multiple_of(r * 16, 16), 16)
                total = grad_stage[slot, part, :].astype(F32) + error_stage[slot, part, :].astype(F32)
                combined[pl.ds(pl.multiple_of(t * tile + r * 16, 16), 16), :] = total.astype(BF16)

            sketch[:, tile_span(t)] = sketch_part(t, slice(0, wide))

    lane = lax.broadcasted_iota(jnp.int32, (rank, 2 * rank), 1)
    line = lax.broadcasted_iota(jnp.int32, (rank, 2 * rank), 0)

    def eliminate(begin, end):
        def step(j, carry):
            value = work[...]
            row = work[pl.ds(j, 1), :]
            column = jnp.sum(jnp.where(lane == j + rank, value, 0.0), axis=1, keepdims=True)
            pivot = jnp.sum(jnp.where(lane[0:1] == j + rank, row, 0.0), axis=1, keepdims=True)
            scale = jnp.where(line[:, 0:1] > j, column / pivot, 0.0)
            work[...] = value - scale * row
            return carry

        lax.fori_loop(begin, end, step, 0)

    core_peer, core = shard_peer(0)
    peer_a, bit_a = island_peer(0)
    peer_b, bit_b = island_peer(1)
    quarter, eighth = half_rank // 2, half_rank // 4

    def part(index, size):
        return pl.ds(pl.multiple_of(index * size, size), size)

    def sketch_flow(r):
        span = row_spans[r]
        upper, lower = slice(0, half_rank), slice(half_rank, rank)
        for s in range(island_bits):
            copies = (
                send(sketch.at[upper, span], sketch_in.at[s, upper, span], island_peer(s)[0]),
                send(sketch.at[lower, span], sketch_in.at[s, lower, span], island_peer(island_bits - 1 - s)[0]),
            )
            yield
            for copy in copies:
                copy.wait()
            sketch[:, span] += sketch_in[s, :, span]
        high, low = split(sketch[:, span])
        sketch_parts[0:rank, span] = high
        sketch_parts[rank:, span] = low

    def gram_flow():
        for s in range(shard_bits):
            copy = send(gram, gram_in.at[s], shard_peer(s)[0])
            yield
            copy.wait()
            gram[...] += gram_in[s]

    def factor_flow(c):
        cols = columns[c]
        middle = (cols.start + cols.stop) // 2
        left, right = slice(cols.start, middle), slice(middle, cols.stop)
        own, other = part(core, half_rank), part(1 - core, half_rank)

        copy = send(projected.at[other, cols], core_in.at[:, cols], core_peer)
        yield
        copy.wait()
        held[:, cols] = projected[own, cols] + core_in[:, cols]

        copies = (
            send(held.at[part(1 - bit_a, quarter), left], first_in.at[:, left], peer_a),
            send(held.at[part(1 - bit_b, quarter), right], first_in.at[:, right], peer_b),
        )
        yield
        for copy in copies:
            copy.wait()
        first[:, left] = held[part(bit_a, quarter), left] + first_in[:, left]
        first[:, right] = held[part(bit_b, quarter), right] + first_in[:, right]

        copies = (
            send(first.at[part(1 - bit_b, eighth), left], second_in.at[:, left], peer_b),
            send(first.at[part(1 - bit_a, eighth), right], second_in.at[:, right], peer_a),
        )
        yield
        for copy in copies:
            copy.wait()
        second[:, left] = first[part(bit_b, eighth), left] + second_in[:, left]
        second[:, right] = first[part(bit_a, eighth), right] + second_in[:, right]

        if shard_bits > 1:
            size = middle - cols.start
            near, bit = shard_peer(1)
            kept = pl.ds(pl.multiple_of(cols.start + bit * size, size), size)
            given = pl.ds(pl.multiple_of(cols.start + (1 - bit) * size, size), size)
            copy = send(second.at[:, given], line_in.at[0, :, given], near)
            yield
            copy.wait()
            second[:, kept] += line_in[0, :, kept]
            for s in range(2, shard_bits):
                copy = send(second.at[:, kept], line_in.at[s - 1, :, kept], shard_peer(s)[0])
                yield
                copy.wait()
                second[:, kept] += line_in[s - 1, :, kept]
            second_all[:, kept] = second[:, kept]
            copy = send(second.at[:, kept], second_all.at[:, kept], near)
            yield
            copy.wait()
        else:
            second_all[:, cols] = second[:, cols]

        first_all[part(bit_b, eighth), left] = second_all[:, left]
        first_all[part(bit_a, eighth), right] = second_all[:, right]
        copies = (
            send(second_all.at[:, left], first_all.at[part(bit_b, eighth), left], peer_b),
            send(second_all.at[:, right], first_all.at[part(bit_a, eighth), right], peer_a),
        )
        yield
        for copy in copies:
            copy.wait()

        held_all[part(bit_a, quarter), left] = first_all[:, left]
        held_all[part(bit_b, quarter), right] = first_all[:, right]
        copies = (
            send(first_all.at[:, left], held_all.at[part(bit_a, quarter), left], peer_a),
            send(first_all.at[:, right], held_all.at[part(bit_b, quarter), right], peer_b),
        )
        yield
        for copy in copies:
            copy.wait()

        projected_all[own, cols] = held_all[:, cols]
        copy = send(held_all.at[:, cols], projected_all.at[own, cols], core_peer)
        yield
        copy.wait()

    def resume(flow):
        return next(flow, True) is None

    def project(r, c):
        @pl.loop(*chunk_strips[c])
        def _(s):
            span = strip_span(s)
            both = jnp.dot(sketch_parts[:, row_spans[r]], combined[row_spans[r], span], preferred_element_type=F32)
            total = both[0:rank] + both[rank:]
            projected[:, span] = total if r == 0 else projected[:, span] + total

    def iteration(sweep, carry):
        counter[0] = 0
        flows = []
        for r, (begin, end) in enumerate(row_chunks):

            @pl.when(sweep == 0)
            def _():
                stream(begin, end)

            @pl.when(sweep > 0)
            def _():
                @pl.loop(begin, end)
                def _(t):
                    sketch[:, tile_span(t)] += sketch_part(t, columns[1])

            flows.append(sketch_flow(r))
            resume(flows[r])

        @pl.when(sweep == 0)
        def _():
            keep.start()

        for s in range(1, island_bits):
            for flow in flows:
                resume(flow)
        last = len(flows) - 1
        for r, flow in enumerate(flows):
            resume(flow)
            if r < last:
                project(r, 0)
                project(r, 1)

        value = sketch[...]
        gram[...] = lax.dot_general(
            value,
            jnp.concatenate([value, value], axis=0),
            (((1,), (1,)), ((), ())),
            precision=HIGH,
            preferred_element_type=F32,
        )
        grams = gram_flow()
        resume(grams)
        halves = [factor_flow(0), factor_flow(1)]
        project(last, 0)
        resume(halves[0])
        more = resume(grams)
        project(last, 1)
        resume(halves[1])
        at = 0
        while more:
            more = resume(grams)
            if at < 2:
                resume(halves[at])
                at += 1
        while at < 2:
            resume(halves[at])
            at += 1
        work[...] = jnp.where(lane < rank, jnp.where(lane == line, 1.0, 0.0), gram[...])

        left_stages = 6 + (shard_bits - 1 if shard_bits > 1 else -1)
        slots = 2 * left_stages - 1
        place = 0
        more = True
        while more:
            for half in halves:
                if place < slots:
                    eliminate(rank * place // slots, rank * (place + 1) // slots)
                place += 1
                more = resume(half)
                if not more:
                    break
        if place < slots:
            eliminate(rank * place // slots, rank)
        inverse = inverse_factor()
        gathered(sweep, inverse, 0)

        @pl.when(sweep < ITERS - 1)
        def _():
            @pl.loop(0, tiles)
            def _(t):
                sketch[:, tile_span(t)] = sketch_part(t, columns[0])

        @pl.when(sweep == ITERS - 1)
        def _():
            orthonormal = jnp.dot(inverse, sketch[...], precision=HIGH, preferred_element_type=F32)
            high, low = split(orthonormal)
            left_out[0:rank, :] = high
            left_out[rank : 2 * rank, :] = high
            left_out[2 * rank :, :] = low

        while resume(halves[1]):
            pass
        gathered(sweep, inverse, 1)
        return carry

    def inverse_factor():
        value = work[...]
        diagonal = jnp.sum(jnp.where(lane == line + rank, value, 0.0), axis=1, keepdims=True)
        return (value * (1.0 / jnp.sqrt(diagonal)))[:, 0:rank]

    def gathered(sweep, inverse, c):
        @pl.loop(*chunk_strips[c])
        def _(s):
            span = strip_span(s)
            basis = jnp.dot(inverse, projected_all[:, span], precision=HIGH, preferred_element_type=F32)

            @pl.when(sweep < ITERS - 1)
            def _():
                high, low = split(basis)
                basis_parts[0:rank, span] = high
                basis_parts[rank:, span] = low

            @pl.when(sweep == ITERS - 1)
            def _():
                high, low = split(basis * (1.0 / islands))
                right_out[0:rank, span] = high
                right_out[rank : 2 * rank, span] = low
                right_out[2 * rank :, span] = high

    keep = pltpu.make_async_copy(combined, combined_out, out_sem)
    lax.fori_loop(0, ITERS, iteration, 0)
    keep.wait()


def outer_kernel(combined_ref, left_ref, right_ref, params_ref, momentum_ref, error_out, params_out, momentum_out):
    tall = combined_ref.shape[0]
    approx = jnp.dot(left_ref[0], right_ref[...], preferred_element_type=F32)
    error_out[0] = (combined_ref[...].astype(F32) - approx[0:tall]).astype(BF16)
    own = approx[tall:]
    new_momentum = momentum_coef * momentum_ref[...] + own
    momentum_out[...] = new_momentum
    params_out[...] = params_ref[...] - outer_rate * (own + momentum_coef * new_momentum)


def steps_of(rows, quarter):
    for steps in (14, 7, 4, 2):
        if rows % (16 * steps) == 0 and quarter % (8 * steps) == 0:
            return steps
    return 1


def shards(islands, shard_count, pseudo_grad, error_buffer, basis_init, params, momentum):
    _, rows, wide = pseudo_grad.shape
    rank = basis_init.shape[1]
    quarter = params.shape[0]
    half, tile = rank // 2, tile_of(rows, 256)
    island_bits, shard_bits = bits_of(islands), bits_of(shard_count)
    sends = 4 * island_bits + shard_bits + 2 * (10 + shard_bits)
    vmem = pl.BlockSpec(memory_space=pltpu.VMEM)
    hbm = pl.BlockSpec(memory_space=pl.ANY)
    combined, left, right = pl.pallas_call(
        functools.partial(power_kernel, islands, shard_count),
        out_shape=(
            jax.ShapeDtypeStruct((rows, wide), BF16),
            jax.ShapeDtypeStruct((3 * rank, rows), BF16),
            jax.ShapeDtypeStruct((3 * rank, wide), BF16),
        ),
        in_specs=[hbm, hbm, vmem],
        out_specs=(hbm, vmem, vmem),
        scratch_shapes=[
            pltpu.VMEM((rows, wide), BF16),
            pltpu.VMEM((2, tile, wide), BF16),
            pltpu.VMEM((2, tile, wide), BF16),
            pltpu.VMEM((2 * rank, wide), BF16),
            pltpu.VMEM((rank, rows), F32),
            pltpu.VMEM((island_bits, rank, rows), F32),
            pltpu.VMEM((2 * rank, rows), BF16),
            pltpu.VMEM((rank, 2 * rank), F32),
            pltpu.VMEM((shard_bits, rank, 2 * rank), F32),
            pltpu.VMEM((rank, 2 * rank), F32),
            pltpu.VMEM((rank, wide), F32),
            pltpu.VMEM((half, wide), F32),
            pltpu.VMEM((half, wide), F32),
            pltpu.VMEM((half // 2, wide), F32),
            pltpu.VMEM((half // 2, wide), F32),
            pltpu.VMEM((half // 4, wide), F32),
            pltpu.VMEM((half // 4, wide), F32),
            pltpu.VMEM((max(shard_bits - 1, 1), half // 4, wide), F32),
            pltpu.VMEM((half // 4, wide), F32),
            pltpu.VMEM((half // 2, wide), F32),
            pltpu.VMEM((half, wide), F32),
            pltpu.VMEM((rank, wide), F32),
            pltpu.SemaphoreType.DMA((2, 2)),
            pltpu.SemaphoreType.DMA,
            pltpu.SemaphoreType.DMA((sends,)),
            pltpu.SemaphoreType.DMA((sends,)),
        ],
        compiler_params=pltpu.CompilerParams(
            collective_id=0, has_side_effects=True, vmem_limit_bytes=56 * 1024 * 1024
        ),
        name="power_iterations",
    )(pseudo_grad, error_buffer, basis_init.T)

    left = left.T
    steps = steps_of(rows, quarter)
    own_left = lax.dynamic_slice_in_dim(left, lax.axis_index("island") * quarter, quarter, 0)
    tall, short = rows // steps, quarter // steps
    left = jnp.concatenate(
        [left.reshape(steps, tall, 3 * rank), own_left.reshape(steps, short, 3 * rank)], axis=1
    )
    new_error, new_params, new_momentum = pl.pallas_call(
        outer_kernel,
        grid=(steps,),
        out_shape=(
            jax.ShapeDtypeStruct((1, rows, wide), BF16),
            jax.ShapeDtypeStruct((quarter, wide), F32),
            jax.ShapeDtypeStruct((quarter, wide), F32),
        ),
        in_specs=[
            pl.BlockSpec((tall, wide), lambda i: (i, 0)),
            pl.BlockSpec((1, tall + short, 3 * rank), lambda i: (i, 0, 0)),
            pl.BlockSpec((3 * rank, wide), lambda i: (0, 0)),
            pl.BlockSpec((short, wide), lambda i: (i, 0)),
            pl.BlockSpec((short, wide), lambda i: (i, 0)),
        ],
        out_specs=(
            pl.BlockSpec((1, tall, wide), lambda i: (0, i, 0)),
            pl.BlockSpec((short, wide), lambda i: (i, 0)),
            pl.BlockSpec((short, wide), lambda i: (i, 0)),
        ),
        compiler_params=pltpu.CompilerParams(vmem_limit_bytes=48 * 1024 * 1024),
        name="outer_step",
    )(combined, left, right, params, momentum)
    return (new_error, new_params, new_momentum)


def solution(mesh):
    placed = (
        P("island", "fsdp", None),
        P("island", "fsdp", None),
        P(),
        P(("fsdp", "island"), None),
        P(("fsdp", "island"), None),
    )
    return jax.shard_map(
        functools.partial(shards, mesh.shape["island"], mesh.shape["fsdp"]),
        mesh=mesh,
        in_specs=placed,
        out_specs=(
            P("island", "fsdp", None),
            P(("fsdp", "island"), None),
            P(("fsdp", "island"), None),
        ),
        check_vma=False,
    )
```

```python
import functools

import jax
import jax.numpy as jnp
from jax import lax
from jax.experimental import pallas as pl
from jax.experimental.pallas import tpu as pltpu
from jax.sharding import PartitionSpec as P

ITERS = 4

momentum_coef = 0.9
outer_rate = 0.7

MESH = pl.DeviceIdType.MESH
F32 = jnp.float32
BF16 = jnp.bfloat16
HIGH = lax.Precision.HIGHEST


def split(value):
    high = value.astype(BF16)
    low = (value - high.astype(F32)).astype(BF16)
    return high, low


def pair(twice):
    high = twice.astype(BF16).astype(F32)
    lane = lax.broadcasted_iota(jnp.int32, twice.shape, 1)
    return jnp.where(lane < twice.shape[1] // 2, high, twice - high).astype(BF16)


def bits_of(extent):
    return extent.bit_length() - 1


def tile_of(extent, want):
    return want if extent % want == 0 else extent


def partner_of(index, bit):
    stride = 1 << bit
    own = (index // stride) % 2
    return index + (1 - 2 * own) * stride, own


def power_kernel(
    islands,
    shards,
    grad_ref,
    error_ref,
    basis_ref,
    combined_out,
    left_out,
    right_out,
    combined,
    grad_stage,
    error_stage,
    basis_parts,
    sketch,
    sketch_in,
    sketch_parts,
    gram,
    gram_in,
    work,
    projected,
    core_in,
    held,
    first_in,
    first,
    second_in,
    second,
    line_in,
    second_all,
    first_all,
    held_all,
    projected_all,
    stage_sem,
    out_sem,
    send_sem,
    recv_sem,
):
    island = lax.axis_index("island")
    shard = lax.axis_index("fsdp")
    rows, wide = combined.shape
    rank = sketch.shape[0]
    half_rank = rank // 2
    island_bits, shard_bits = bits_of(islands), bits_of(shards)

    def island_peer(bit):
        index, own = partner_of(island, bit)
        return (index, shard), own

    def shard_peer(bit):
        index, own = partner_of(shard, bit)
        return (island, index), own

    peers = [island_peer(b)[0] for b in range(island_bits)] + [shard_peer(b)[0] for b in range(shard_bits)]

    counter = [0]

    def send(src, dst, peer):
        number = counter[0]
        counter[0] += 1
        copy = pltpu.make_async_remote_copy(
            src_ref=src,
            dst_ref=dst,
            send_sem=send_sem.at[number],
            recv_sem=recv_sem.at[number],
            device_id=peer,
            device_id_type=MESH,
        )
        copy.start()
        return copy

    tile = tile_of(rows, 256)
    tiles = rows // tile

    def fetch(t, slot):
        span = pl.ds(pl.multiple_of(t * tile, tile), tile)
        return (
            pltpu.make_async_copy(grad_ref.at[0, span], grad_stage.at[slot], stage_sem.at[0, slot]),
            pltpu.make_async_copy(error_ref.at[0, span], error_stage.at[slot], stage_sem.at[1, slot]),
        )

    for copy in fetch(0, 0):
        copy.start()

    barrier = pltpu.get_barrier_semaphore()
    for peer in peers:
        pl.semaphore_signal(barrier, inc=1, device_id=peer, device_id_type=MESH)
    pl.semaphore_wait(barrier, len(peers))

    strip = tile_of(wide, 512)
    strips = wide // strip

    def strip_span(s):
        return pl.ds(pl.multiple_of(s * strip, strip), strip)

    @pl.loop(0, strips)
    def _(s):
        span = strip_span(s)
        basis_parts[span, :] = pair(basis_ref[span, :])

    cut = (tiles + 1) // 2
    row_chunks = [(0, cut), (cut, tiles)] if tiles > 1 else [(0, 1)]
    row_spans = [slice(begin * tile, end * tile) for begin, end in row_chunks]
    chunk_strips = [(c * strips // 2, (c + 1) * strips // 2) for c in range(2)]
    columns = [slice(begin * strip, end * strip) for begin, end in chunk_strips]

    def tile_span(t):
        return pl.ds(pl.multiple_of(t * tile, tile), tile)

    def sketch_part(t, cols):
        both = jnp.dot(combined[tile_span(t), cols], basis_parts[cols, :], preferred_element_type=F32).T
        return both[0:rank] + both[rank:]

    def stream(begin, end):
        @pl.loop(begin, end)
        def _(t):
            slot = lax.rem(t, 2)

            @pl.when(t + 1 < tiles)
            def _():
                for copy in fetch(t + 1, 1 - slot):
                    copy.start()

            for copy in fetch(t, slot):
                copy.wait()

            @pl.loop(0, tile // 16)
            def _(r):
                part = pl.ds(pl.multiple_of(r * 16, 16), 16)
                total = grad_stage[slot, part, :].astype(F32) + error_stage[slot, part, :].astype(F32)
                combined[pl.ds(pl.multiple_of(t * tile + r * 16, 16), 16), :] = total.astype(BF16)

            sketch[:, tile_span(t)] = sketch_part(t, slice(0, wide))

    lane = lax.broadcasted_iota(jnp.int32, (rank, 2 * rank), 1)
    line = lax.broadcasted_iota(jnp.int32, (rank, 2 * rank), 0)

    def eliminate(begin, end):
        value = work[...]
        for j in range(begin, end):
            column = jnp.broadcast_to(value[:, j + rank : j + rank + 1], value.shape)
            row = value[j : j + 1] / column[j : j + 1]
            value = value - jnp.where(line > j, column, 0.0) * row
        work[...] = value

    core_peer, core = shard_peer(0)
    peer_a, bit_a = island_peer(0)
    peer_b, bit_b = island_peer(1)
    quarter, eighth = half_rank // 2, half_rank // 4

    def part(index, size):
        return pl.ds(pl.multiple_of(index * size, size), size)

    def sketch_flow(r):
        span = row_spans[r]
        upper, lower = slice(0, half_rank), slice(half_rank, rank)
        for s in range(island_bits):
            copies = (
                send(sketch.at[upper, span], sketch_in.at[s, upper, span], island_peer(s)[0]),
                send(sketch.at[lower, span], sketch_in.at[s, lower, span], island_peer(island_bits - 1 - s)[0]),
            )
            yield
            for copy in copies:
                copy.wait()
            sketch[:, span] += sketch_in[s, :, span]
        high, low = split(sketch[:, span])
        sketch_parts[0:rank, span] = high
        sketch_parts[rank:, span] = low

    def gram_flow():
        for s in range(shard_bits):
            copy = send(gram, gram_in.at[s], shard_peer(s)[0])
            yield
            copy.wait()
            gram[...] += gram_in[s]

    def factor_flow(c):
        cols = columns[c]
        middle = (cols.start + cols.stop) // 2
        left, right = slice(cols.start, middle), slice(middle, cols.stop)
        own, other = part(core, half_rank), part(1 - core, half_rank)

        copy = send(projected.at[other, cols], core_in.at[:, cols], core_peer)
        yield
        copy.wait()
        held[:, cols] = projected[own, cols] + core_in[:, cols]

        copies = (
            send(held.at[part(1 - bit_a, quarter), left], first_in.at[:, left], peer_a),
            send(held.at[part(1 - bit_b, quarter), right], first_in.at[:, right], peer_b),
        )
        yield
        for copy in copies:
            copy.wait()
        first[:, left] = held[part(bit_a, quarter), left] + first_in[:, left]
        first[:, right] = held[part(bit_b, quarter), right] + first_in[:, right]

        copies = (
            send(first.at[part(1 - bit_b, eighth), left], second_in.at[:, left], peer_b),
            send(first.at[part(1 - bit_a, eighth), right], second_in.at[:, right], peer_a),
        )
        yield
        for copy in copies:
            copy.wait()
        second[:, left] = first[part(bit_b, eighth), left] + second_in[:, left]
        second[:, right] = first[part(bit_a, eighth), right] + second_in[:, right]

        if shard_bits > 1:
            size = middle - cols.start
            near, bit = shard_peer(1)
            kept = pl.ds(pl.multiple_of(cols.start + bit * size, size), size)
            given = pl.ds(pl.multiple_of(cols.start + (1 - bit) * size, size), size)
            copy = send(second.at[:, given], line_in.at[0, :, given], near)
            yield
            copy.wait()
            second[:, kept] += line_in[0, :, kept]
            for s in range(2, shard_bits):
                copy = send(second.at[:, kept], line_in.at[s - 1, :, kept], shard_peer(s)[0])
                yield
                copy.wait()
                second[:, kept] += line_in[s - 1, :, kept]
            second_all[:, kept] = second[:, kept]
            copy = send(second.at[:, kept], second_all.at[:, kept], near)
            yield
            copy.wait()
        else:
            second_all[:, cols] = second[:, cols]

        first_all[part(bit_b, eighth), left] = second_all[:, left]
        first_all[part(bit_a, eighth), right] = second_all[:, right]
        copies = (
            send(second_all.at[:, left], first_all.at[part(bit_b, eighth), left], peer_b),
            send(second_all.at[:, right], first_all.at[part(bit_a, eighth), right], peer_a),
        )
        yield
        for copy in copies:
            copy.wait()

        held_all[part(bit_a, quarter), left] = first_all[:, left]
        held_all[part(bit_b, quarter), right] = first_all[:, right]
        copies = (
            send(first_all.at[:, left], held_all.at[part(bit_a, quarter), left], peer_a),
            send(first_all.at[:, right], held_all.at[part(bit_b, quarter), right], peer_b),
        )
        yield
        for copy in copies:
            copy.wait()

        projected_all[own, cols] = held_all[:, cols]
        copy = send(held_all.at[:, cols], projected_all.at[own, cols], core_peer)
        yield
        copy.wait()

    def resume(flow):
        return next(flow, True) is None

    def project(r, c):
        @pl.loop(*chunk_strips[c])
        def _(s):
            span = strip_span(s)
            both = jnp.dot(sketch_parts[:, row_spans[r]], combined[row_spans[r], span], preferred_element_type=F32)
            total = both[0:rank] + both[rank:]
            projected[:, span] = total if r == 0 else projected[:, span] + total

    def iteration(sweep, carry):
        counter[0] = 0
        flows = []
        for r, (begin, end) in enumerate(row_chunks):

            @pl.when(sweep == 0)
            def _():
                stream(begin, end)

            @pl.when(sweep > 0)
            def _():
                @pl.loop(begin, end)
                def _(t):
                    sketch[:, tile_span(t)] += sketch_part(t, columns[1])

            flows.append(sketch_flow(r))
            resume(flows[r])

        @pl.when(sweep == 0)
        def _():
            keep.start()

        for s in range(1, island_bits):
            for flow in flows:
                resume(flow)
        last = len(flows) - 1
        for r, flow in enumerate(flows):
            resume(flow)
            value = sketch[:, row_spans[r]]
            square = lax.dot_general(
                value,
                jnp.concatenate([value, value], axis=0),
                (((1,), (1,)), ((), ())),
                precision=HIGH,
                preferred_element_type=F32,
            )
            gram[...] = square if r == 0 else gram[...] + square
            if r < last:
                project(r, 0)
                project(r, 1)

        grams = gram_flow()
        resume(grams)
        halves = [factor_flow(0), factor_flow(1)]
        project(last, 0)
        resume(halves[0])
        more = resume(grams)
        project(last, 1)
        resume(halves[1])
        at = 0
        while more:
            more = resume(grams)
            if at < 2:
                resume(halves[at])
                at += 1
        while at < 2:
            resume(halves[at])
            at += 1
        work[...] = jnp.where(lane < rank, jnp.where(lane == line, 1.0, 0.0), gram[...])

        left_stages = 6 + (shard_bits - 1 if shard_bits > 1 else -1)
        slots = 2 * left_stages - 1
        place = 0
        more = True
        while more:
            for half in halves:
                if place < slots:
                    eliminate(rank * place // slots, rank * (place + 1) // slots)
                place += 1
                more = resume(half)
                if not more:
                    break
        if place < slots:
            eliminate(rank * place // slots, rank)
        inverse = inverse_factor()
        gathered(sweep, inverse, 0)

        @pl.when(sweep < ITERS - 1)
        def _():
            @pl.loop(0, tiles)
            def _(t):
                sketch[:, tile_span(t)] = sketch_part(t, columns[0])

        @pl.when(sweep == ITERS - 1)
        def _():
            thrice = lax.dot_general(
                sketch[...].T,
                jnp.concatenate([inverse] * 3, axis=0),
                (((1,), (1,)), ((), ())),
                precision=HIGH,
                preferred_element_type=F32,
            )
            high = thrice.astype(BF16).astype(F32)
            spot = lax.broadcasted_iota(jnp.int32, thrice.shape, 1)
            left_out[...] = jnp.where(spot < 2 * rank, high, thrice - high).astype(BF16)

        while resume(halves[1]):
            pass
        gathered(sweep, inverse, 1)
        return carry

    def inverse_factor():
        value = work[...]
        diagonal = jnp.sum(jnp.where(lane == line + rank, value, 0.0), axis=1, keepdims=True)
        return (value * (1.0 / jnp.sqrt(diagonal)))[:, 0:rank]

    def gathered(sweep, inverse, c):
        @pl.when(sweep < ITERS - 1)
        def _():
            weight_high, weight_low = split(jnp.concatenate([inverse, inverse], axis=0))

            @pl.loop(*chunk_strips[c])
            def _(s):
                span = strip_span(s)
                high, low = split(projected_all[:, span].T)

                def product(one, two):
                    return lax.dot_general(one, two, (((1,), (1,)), ((), ())), preferred_element_type=F32)

                twice = product(high, weight_high) + (product(high, weight_low) + product(low, weight_high))
                basis_parts[span, :] = pair(twice)

        @pl.when(sweep == ITERS - 1)
        def _():
            @pl.loop(*chunk_strips[c])
            def _(s):
                span = strip_span(s)
                basis = jnp.dot(inverse, projected_all[:, span], precision=HIGH, preferred_element_type=F32)
                high, low = split(basis * (1.0 / islands))
                right_out[0:rank, span] = high
                right_out[rank : 2 * rank, span] = low
                right_out[2 * rank :, span] = high

    keep = pltpu.make_async_copy(combined, combined_out, out_sem)
    lax.fori_loop(0, ITERS, iteration, 0)
    keep.wait()


def outer_kernel(combined_ref, left_ref, right_ref, params_ref, momentum_ref, error_out, params_out, momentum_out):
    tall, short = combined_ref.shape[0], params_ref.shape[0]
    step = pl.program_id(0)
    begin = (lax.axis_index("island") * pl.num_programs(0) + step) * short
    left = jnp.concatenate(
        [left_ref[pl.ds(pl.multiple_of(step * tall, tall), tall), :], left_ref[pl.ds(pl.multiple_of(begin, short), short), :]],
        axis=0,
    )
    approx = jnp.dot(left, right_ref[...], preferred_element_type=F32)
    error_out[0] = (combined_ref[...].astype(F32) - approx[0:tall]).astype(BF16)
    own = approx[tall:]
    new_momentum = momentum_coef * momentum_ref[...] + own
    momentum_out[...] = new_momentum
    params_out[...] = params_ref[...] - outer_rate * (own + momentum_coef * new_momentum)


def steps_of(rows, quarter):
    for steps in (7, 4, 2):
        if rows % (16 * steps) == 0 and quarter % (16 * steps) == 0:
            return steps
    return 1


def shards(islands, shard_count, pseudo_grad, error_buffer, basis_init, params, momentum):
    _, rows, wide = pseudo_grad.shape
    rank = basis_init.shape[1]
    quarter = params.shape[0]
    half, tile = rank // 2, tile_of(rows, 256)
    island_bits, shard_bits = bits_of(islands), bits_of(shard_count)
    sends = 4 * island_bits + shard_bits + 2 * (10 + shard_bits)
    vmem = pl.BlockSpec(memory_space=pltpu.VMEM)
    hbm = pl.BlockSpec(memory_space=pl.ANY)
    combined, left, right = pl.pallas_call(
        functools.partial(power_kernel, islands, shard_count),
        out_shape=(
            jax.ShapeDtypeStruct((rows, wide), BF16),
            jax.ShapeDtypeStruct((rows, 3 * rank), BF16),
            jax.ShapeDtypeStruct((3 * rank, wide), BF16),
        ),
        in_specs=[hbm, hbm, vmem],
        out_specs=(hbm, vmem, vmem),
        scratch_shapes=[
            pltpu.VMEM((rows, wide), BF16),
            pltpu.VMEM((2, tile, wide), BF16),
            pltpu.VMEM((2, tile, wide), BF16),
            pltpu.VMEM((wide, 2 * rank), BF16),
            pltpu.VMEM((rank, rows), F32),
            pltpu.VMEM((island_bits, rank, rows), F32),
            pltpu.VMEM((2 * rank, rows), BF16),
            pltpu.VMEM((rank, 2 * rank), F32),
            pltpu.VMEM((shard_bits, rank, 2 * rank), F32),
            pltpu.VMEM((rank, 2 * rank), F32),
            pltpu.VMEM((rank, wide), F32),
            pltpu.VMEM((half, wide), F32),
            pltpu.VMEM((half, wide), F32),
            pltpu.VMEM((half // 2, wide), F32),
            pltpu.VMEM((half // 2, wide), F32),
            pltpu.VMEM((half // 4, wide), F32),
            pltpu.VMEM((half // 4, wide), F32),
            pltpu.VMEM((max(shard_bits - 1, 1), half // 4, wide), F32),
            pltpu.VMEM((half // 4, wide), F32),
            pltpu.VMEM((half // 2, wide), F32),
            pltpu.VMEM((half, wide), F32),
            pltpu.VMEM((rank, wide), F32),
            pltpu.SemaphoreType.DMA((2, 2)),
            pltpu.SemaphoreType.DMA,
            pltpu.SemaphoreType.DMA((sends,)),
            pltpu.SemaphoreType.DMA((sends,)),
        ],
        compiler_params=pltpu.CompilerParams(
            collective_id=0, has_side_effects=True, vmem_limit_bytes=56 * 1024 * 1024
        ),
        name="power_iterations",
    )(pseudo_grad, error_buffer, jnp.concatenate([basis_init, basis_init], axis=1))

    steps = steps_of(rows, quarter)
    tall, short = rows // steps, quarter // steps
    new_error, new_params, new_momentum = pl.pallas_call(
        outer_kernel,
        grid=(steps,),
        out_shape=(
            jax.ShapeDtypeStruct((1, rows, wide), BF16),
            jax.ShapeDtypeStruct((quarter, wide), F32),
            jax.ShapeDtypeStruct((quarter, wide), F32),
        ),
        in_specs=[
            pl.BlockSpec((tall, wide), lambda i: (i, 0)),
            pl.BlockSpec((rows, 3 * rank), lambda i: (0, 0)),
            pl.BlockSpec((3 * rank, wide), lambda i: (0, 0)),
            pl.BlockSpec((short, wide), lambda i: (i, 0)),
            pl.BlockSpec((short, wide), lambda i: (i, 0)),
        ],
        out_specs=(
            pl.BlockSpec((1, tall, wide), lambda i: (0, i, 0)),
            pl.BlockSpec((short, wide), lambda i: (i, 0)),
            pl.BlockSpec((short, wide), lambda i: (i, 0)),
        ),
        compiler_params=pltpu.CompilerParams(vmem_limit_bytes=48 * 1024 * 1024),
        name="outer_step",
    )(combined, left, right, params, momentum)
    return (new_error, new_params, new_momentum)


def solution(mesh):
    placed = (
        P("island", "fsdp", None),
        P("island", "fsdp", None),
        P(),
        P(("fsdp", "island"), None),
        P(("fsdp", "island"), None),
    )
    return jax.shard_map(
        functools.partial(shards, mesh.shape["island"], mesh.shape["fsdp"]),
        mesh=mesh,
        in_specs=placed,
        out_specs=(
            P("island", "fsdp", None),
            P(("fsdp", "island"), None),
            P(("fsdp", "island"), None),
        ),
        check_vma=False,
    )
```

```python
import functools

import jax
import jax.numpy as jnp
from jax import lax
from jax.experimental import pallas as pl
from jax.experimental.pallas import tpu as pltpu
from jax.sharding import PartitionSpec as P

ITERS = 4

momentum_coef = 0.9
outer_rate = 0.7

MESH = pl.DeviceIdType.MESH
F32 = jnp.float32
BF16 = jnp.bfloat16
HIGH = lax.Precision.HIGHEST


def split(value):
    high = value.astype(BF16)
    low = (value - high.astype(F32)).astype(BF16)
    return high, low


def bits_of(extent):
    return extent.bit_length() - 1


def tile_of(extent, want):
    return want if extent % want == 0 else extent


def partner_of(index, bit):
    stride = 1 << bit
    own = (index // stride) % 2
    return index + (1 - 2 * own) * stride, own


def power_kernel(
    islands,
    shards,
    grad_ref,
    error_ref,
    basis_ref,
    combined_out,
    left_out,
    right_out,
    combined,
    grad_stage,
    error_stage,
    basis_parts,
    sketch,
    sketch_in,
    sketch_parts,
    gram,
    gram_in,
    work,
    projected,
    core_in,
    held,
    first_in,
    first,
    second_in,
    second,
    line_in,
    second_all,
    first_all,
    held_all,
    projected_all,
    stage_sem,
    out_sem,
    send_sem,
    recv_sem,
):
    island = lax.axis_index("island")
    shard = lax.axis_index("fsdp")
    rows, wide = combined.shape
    rank = sketch.shape[0]
    half_rank = rank // 2
    island_bits, shard_bits = bits_of(islands), bits_of(shards)

    def island_peer(bit):
        index, own = partner_of(island, bit)
        return (index, shard), own

    def shard_peer(bit):
        index, own = partner_of(shard, bit)
        return (island, index), own

    peers = [island_peer(b)[0] for b in range(island_bits)] + [shard_peer(b)[0] for b in range(shard_bits)]

    counter = [0]

    def send(src, dst, peer):
        number = counter[0]
        counter[0] += 1
        copy = pltpu.make_async_remote_copy(
            src_ref=src,
            dst_ref=dst,
            send_sem=send_sem.at[number],
            recv_sem=recv_sem.at[number],
            device_id=peer,
            device_id_type=MESH,
        )
        copy.start()
        return copy

    tile = tile_of(rows, 256)
    tiles = rows // tile

    def fetch(t, slot):
        span = pl.ds(pl.multiple_of(t * tile, tile), tile)
        return (
            pltpu.make_async_copy(grad_ref.at[0, span], grad_stage.at[slot], stage_sem.at[0, slot]),
            pltpu.make_async_copy(error_ref.at[0, span], error_stage.at[slot], stage_sem.at[1, slot]),
        )

    for copy in fetch(0, 0):
        copy.start()

    barrier = pltpu.get_barrier_semaphore()
    for peer in peers:
        pl.semaphore_signal(barrier, inc=1, device_id=peer, device_id_type=MESH)
    pl.semaphore_wait(barrier, len(peers))

    strip = tile_of(wide, 512)
    strips = wide // strip

    def strip_span(s):
        return pl.ds(pl.multiple_of(s * strip, strip), strip)

    @pl.loop(0, strips)
    def _(s):
        span = strip_span(s)
        high, low = split(basis_ref[:, span])
        basis_parts[0:rank, span] = high
        basis_parts[rank:, span] = low

    cut = (tiles + 1) // 2
    row_chunks = [(0, cut), (cut, tiles)] if tiles > 1 else [(0, 1)]
    row_spans = [slice(begin * tile, end * tile) for begin, end in row_chunks]
    chunk_strips = [(c * strips // 2, (c + 1) * strips // 2) for c in range(2)]
    columns = [slice(begin * strip, end * strip) for begin, end in chunk_strips]

    def tile_span(t):
        return pl.ds(pl.multiple_of(t * tile, tile), tile)

    def sketch_part(t, cols):
        both = lax.dot_general(
            basis_parts[:, cols],
            combined[tile_span(t), cols],
            (((1,), (1,)), ((), ())),
            preferred_element_type=F32,
        )
        return both[0:rank] + both[rank:]

    def stream(begin, end):
        @pl.loop(begin, end)
        def _(t):
            slot = lax.rem(t, 2)

            @pl.when(t + 1 < tiles)
            def _():
                for copy in fetch(t + 1, 1 - slot):
                    copy.start()

            for copy in fetch(t, slot):
                copy.wait()

            @pl.loop(0, tile // 16)
            def _(r):
                part = pl.ds(pl.multiple_of(r * 16, 16), 16)
                total = grad_stage[slot, part, :].astype(F32) + error_stage[slot, part, :].astype(F32)
                combined[pl.ds(pl.multiple_of(t * tile + r * 16, 16), 16), :] = total.astype(BF16)

            sketch[:, tile_span(t)] = sketch_part(t, slice(0, wide))

    lane = lax.broadcasted_iota(jnp.int32, (rank, 2 * rank), 1)
    line = lax.broadcasted_iota(jnp.int32, (rank, 2 * rank), 0)

    def eliminate(begin, end):
        value = work[...]
        for j in range(begin, end):
            column = jnp.broadcast_to(value[:, j + rank : j + rank + 1], value.shape)
            row = value[j : j + 1] / column[j : j + 1]
            value = value - jnp.where(line > j, column, 0.0) * row
        work[...] = value

    core_peer, core = shard_peer(0)
    peer_a, bit_a = island_peer(0)
    peer_b, bit_b = island_peer(1)
    quarter, eighth = half_rank // 2, half_rank // 4

    def part(index, size):
        return pl.ds(pl.multiple_of(index * size, size), size)

    def sketch_flow(r):
        span = row_spans[r]
        upper, lower = slice(0, half_rank), slice(half_rank, rank)
        for s in range(island_bits):
            copies = (
                send(sketch.at[upper, span], sketch_in.at[s, upper, span], island_peer(s)[0]),
                send(sketch.at[lower, span], sketch_in.at[s, lower, span], island_peer(island_bits - 1 - s)[0]),
            )
            yield
            for copy in copies:
                copy.wait()
            sketch[:, span] += sketch_in[s, :, span]
        high, low = split(sketch[:, span])
        sketch_parts[0:rank, span] = high
        sketch_parts[rank:, span] = low

    def gram_flow():
        for s in range(shard_bits):
            copy = send(gram, gram_in.at[s], shard_peer(s)[0])
            yield
            copy.wait()
            gram[...] += gram_in[s]

    def factor_flow(c):
        cols = columns[c]
        middle = (cols.start + cols.stop) // 2
        left, right = slice(cols.start, middle), slice(middle, cols.stop)
        own, other = part(core, half_rank), part(1 - core, half_rank)

        copy = send(projected.at[other, cols], core_in.at[:, cols], core_peer)
        yield
        copy.wait()
        held[:, cols] = projected[own, cols] + core_in[:, cols]

        copies = (
            send(held.at[part(1 - bit_a, quarter), left], first_in.at[:, left], peer_a),
            send(held.at[part(1 - bit_b, quarter), right], first_in.at[:, right], peer_b),
        )
        yield
        for copy in copies:
            copy.wait()
        first[:, left] = held[part(bit_a, quarter), left] + first_in[:, left]
        first[:, right] = held[part(bit_b, quarter), right] + first_in[:, right]

        copies = (
            send(first.at[part(1 - bit_b, eighth), left], second_in.at[:, left], peer_b),
            send(first.at[part(1 - bit_a, eighth), right], second_in.at[:, right], peer_a),
        )
        yield
        for copy in copies:
            copy.wait()
        second[:, left] = first[part(bit_b, eighth), left] + second_in[:, left]
        second[:, right] = first[part(bit_a, eighth), right] + second_in[:, right]

        if shard_bits > 1:
            size = middle - cols.start
            near, bit = shard_peer(1)
            kept = pl.ds(pl.multiple_of(cols.start + bit * size, size), size)
            given = pl.ds(pl.multiple_of(cols.start + (1 - bit) * size, size), size)
            copy = send(second.at[:, given], line_in.at[0, :, given], near)
            yield
            copy.wait()
            second[:, kept] += line_in[0, :, kept]
            for s in range(2, shard_bits):
                copy = send(second.at[:, kept], line_in.at[s - 1, :, kept], shard_peer(s)[0])
                yield
                copy.wait()
                second[:, kept] += line_in[s - 1, :, kept]
            second_all[:, kept] = second[:, kept]
            copy = send(second.at[:, kept], second_all.at[:, kept], near)
            yield
            copy.wait()
        else:
            second_all[:, cols] = second[:, cols]

        first_all[part(bit_b, eighth), left] = second_all[:, left]
        first_all[part(bit_a, eighth), right] = second_all[:, right]
        copies = (
            send(second_all.at[:, left], first_all.at[part(bit_b, eighth), left], peer_b),
            send(second_all.at[:, right], first_all.at[part(bit_a, eighth), right], peer_a),
        )
        yield
        for copy in copies:
            copy.wait()

        held_all[part(bit_a, quarter), left] = first_all[:, left]
        held_all[part(bit_b, quarter), right] = first_all[:, right]
        copies = (
            send(first_all.at[:, left], held_all.at[part(bit_a, quarter), left], peer_a),
            send(first_all.at[:, right], held_all.at[part(bit_b, quarter), right], peer_b),
        )
        yield
        for copy in copies:
            copy.wait()

        projected_all[own, cols] = held_all[:, cols]
        copy = send(held_all.at[:, cols], projected_all.at[own, cols], core_peer)
        yield
        copy.wait()

    def resume(flow):
        return next(flow, True) is None

    def project(r, c):
        @pl.loop(*chunk_strips[c])
        def _(s):
            span = strip_span(s)
            both = jnp.dot(sketch_parts[:, row_spans[r]], combined[row_spans[r], span], preferred_element_type=F32)
            total = both[0:rank] + both[rank:]
            projected[:, span] = total if r == 0 else projected[:, span] + total

    def iteration(sweep, carry):
        counter[0] = 0
        flows = []
        for r, (begin, end) in enumerate(row_chunks):

            @pl.when(sweep == 0)
            def _():
                stream(begin, end)

            @pl.when(sweep > 0)
            def _():
                @pl.loop(begin, end)
                def _(t):
                    sketch[:, tile_span(t)] += sketch_part(t, columns[1])

            flows.append(sketch_flow(r))
            resume(flows[r])

        @pl.when(sweep == 0)
        def _():
            keep.start()

        for s in range(1, island_bits):
            for flow in flows:
                resume(flow)
        last = len(flows) - 1
        for r, flow in enumerate(flows):
            resume(flow)
            value = sketch[:, row_spans[r]]
            square = lax.dot_general(
                value,
                jnp.concatenate([value, value], axis=0),
                (((1,), (1,)), ((), ())),
                precision=HIGH,
                preferred_element_type=F32,
            )
            gram[...] = square if r == 0 else gram[...] + square
            if r < last:
                project(r, 0)
                project(r, 1)

        grams = gram_flow()
        resume(grams)
        halves = [factor_flow(0), factor_flow(1)]
        project(last, 0)
        resume(halves[0])
        more = resume(grams)
        project(last, 1)
        resume(halves[1])
        resume(halves[0])
        while more:
            more = resume(grams)
        work[...] = jnp.where(lane < rank, jnp.where(lane == line, 1.0, 0.0), gram[...])

        ahead = rank // 8
        eliminate(0, ahead)
        resume(halves[0])
        slots = 2 * (6 + (shard_bits if shard_bits > 1 else 0) - 2)
        place = 0
        more = True
        while more:
            for half in (halves[1], halves[0]):
                if place < slots:
                    eliminate(
                        ahead + (rank - ahead) * place // slots, ahead + (rank - ahead) * (place + 1) // slots
                    )
                place += 1
                more = resume(half)
        if place < slots:
            eliminate(ahead + (rank - ahead) * place // slots, rank)
        inverse = inverse_factor()
        gathered(sweep, inverse, 0)

        for begin, end in row_chunks:
            resume(halves[1])

            @pl.when(sweep < ITERS - 1)
            def _():
                @pl.loop(begin, end)
                def _(t):
                    sketch[:, tile_span(t)] = sketch_part(t, columns[0])

        @pl.when(sweep == ITERS - 1)
        def _():
            thrice = lax.dot_general(
                sketch[...].T,
                jnp.concatenate([inverse] * 3, axis=0),
                (((1,), (1,)), ((), ())),
                precision=HIGH,
                preferred_element_type=F32,
            )
            high = thrice.astype(BF16).astype(F32)
            spot = lax.broadcasted_iota(jnp.int32, thrice.shape, 1)
            left_out[...] = jnp.where(spot < 2 * rank, high, thrice - high).astype(BF16)

        while resume(halves[1]):
            pass
        gathered(sweep, inverse, 1)
        return carry

    def inverse_factor():
        value = work[...]
        diagonal = jnp.sum(jnp.where(lane == line + rank, value, 0.0), axis=1, keepdims=True)
        return (value * (1.0 / jnp.sqrt(diagonal)))[:, 0:rank]

    def gathered(sweep, inverse, c):
        @pl.when(sweep < ITERS - 1)
        def _():
            weight_high, weight_low = split(inverse)
            weights = jnp.concatenate([weight_high, weight_low], axis=0)

            @pl.loop(*chunk_strips[c])
            def _(s):
                span = strip_span(s)
                high, low = split(projected_all[:, span])
                both = jnp.dot(weights, high, preferred_element_type=F32)
                small = both[rank:] + jnp.dot(weight_high, low, preferred_element_type=F32)
                high, low = split(both[0:rank] + small)
                basis_parts[0:rank, span] = high
                basis_parts[rank:, span] = low

        @pl.when(sweep == ITERS - 1)
        def _():
            @pl.loop(*chunk_strips[c])
            def _(s):
                span = strip_span(s)
                basis = jnp.dot(inverse, projected_all[:, span], precision=HIGH, preferred_element_type=F32)
                high, low = split(basis * (1.0 / islands))
                right_out[0:rank, span] = high
                right_out[rank : 2 * rank, span] = low
                right_out[2 * rank :, span] = high

    keep = pltpu.make_async_copy(combined, combined_out, out_sem)
    lax.fori_loop(0, ITERS, iteration, 0)
    keep.wait()


def outer_kernel(combined_ref, left_ref, right_ref, params_ref, momentum_ref, error_out, params_out, momentum_out):
    tall, short = combined_ref.shape[0], params_ref.shape[0]
    step = pl.program_id(0)
    begin = (lax.axis_index("island") * pl.num_programs(0) + step) * short
    left = jnp.concatenate(
        [left_ref[pl.ds(pl.multiple_of(step * tall, tall), tall), :], left_ref[pl.ds(pl.multiple_of(begin, short), short), :]],
        axis=0,
    )
    approx = jnp.dot(left, right_ref[...], preferred_element_type=F32)
    error_out[0] = (combined_ref[...].astype(F32) - approx[0:tall]).astype(BF16)
    own = approx[tall:]
    new_momentum = momentum_coef * momentum_ref[...] + own
    momentum_out[...] = new_momentum
    params_out[...] = params_ref[...] - outer_rate * (own + momentum_coef * new_momentum)


def steps_of(rows, quarter):
    for steps in (7, 4, 2):
        if rows % (16 * steps) == 0 and quarter % (16 * steps) == 0:
            return steps
    return 1


def shards(islands, shard_count, pseudo_grad, error_buffer, basis_init, params, momentum):
    _, rows, wide = pseudo_grad.shape
    rank = basis_init.shape[1]
    quarter = params.shape[0]
    half, tile = rank // 2, tile_of(rows, 256)
    island_bits, shard_bits = bits_of(islands), bits_of(shard_count)
    sends = 4 * island_bits + shard_bits + 2 * (10 + shard_bits)
    vmem = pl.BlockSpec(memory_space=pltpu.VMEM)
    hbm = pl.BlockSpec(memory_space=pl.ANY)
    combined, left, right = pl.pallas_call(
        functools.partial(power_kernel, islands, shard_count),
        out_shape=(
            jax.ShapeDtypeStruct((rows, wide), BF16),
            jax.ShapeDtypeStruct((rows, 3 * rank), BF16),
            jax.ShapeDtypeStruct((3 * rank, wide), BF16),
        ),
        in_specs=[hbm, hbm, vmem],
        out_specs=(hbm, vmem, vmem),
        scratch_shapes=[
            pltpu.VMEM((rows, wide), BF16),
            pltpu.VMEM((2, tile, wide), BF16),
            pltpu.VMEM((2, tile, wide), BF16),
            pltpu.VMEM((2 * rank, wide), BF16),
            pltpu.VMEM((rank, rows), F32),
            pltpu.VMEM((island_bits, rank, rows), F32),
            pltpu.VMEM((2 * rank, rows), BF16),
            pltpu.VMEM((rank, 2 * rank), F32),
            pltpu.VMEM((shard_bits, rank, 2 * rank), F32),
            pltpu.VMEM((rank, 2 * rank), F32),
            pltpu.VMEM((rank, wide), F32),
            pltpu.VMEM((half, wide), F32),
            pltpu.VMEM((half, wide), F32),
            pltpu.VMEM((half // 2, wide), F32),
            pltpu.VMEM((half // 2, wide), F32),
            pltpu.VMEM((half // 4, wide), F32),
            pltpu.VMEM((half // 4, wide), F32),
            pltpu.VMEM((max(shard_bits - 1, 1), half // 4, wide), F32),
            pltpu.VMEM((half // 4, wide), F32),
            pltpu.VMEM((half // 2, wide), F32),
            pltpu.VMEM((half, wide), F32),
            pltpu.VMEM((rank, wide), F32),
            pltpu.SemaphoreType.DMA((2, 2)),
            pltpu.SemaphoreType.DMA,
            pltpu.SemaphoreType.DMA((sends,)),
            pltpu.SemaphoreType.DMA((sends,)),
        ],
        compiler_params=pltpu.CompilerParams(
            collective_id=0, has_side_effects=True, vmem_limit_bytes=56 * 1024 * 1024
        ),
        name="power_iterations",
    )(pseudo_grad, error_buffer, basis_init.T)

    steps = steps_of(rows, quarter)
    tall, short = rows // steps, quarter // steps
    new_error, new_params, new_momentum = pl.pallas_call(
        outer_kernel,
        grid=(steps,),
        out_shape=(
            jax.ShapeDtypeStruct((1, rows, wide), BF16),
            jax.ShapeDtypeStruct((quarter, wide), F32),
            jax.ShapeDtypeStruct((quarter, wide), F32),
        ),
        in_specs=[
            pl.BlockSpec((tall, wide), lambda i: (i, 0)),
            pl.BlockSpec((rows, 3 * rank), lambda i: (0, 0)),
            pl.BlockSpec((3 * rank, wide), lambda i: (0, 0)),
            pl.BlockSpec((short, wide), lambda i: (i, 0)),
            pl.BlockSpec((short, wide), lambda i: (i, 0)),
        ],
        out_specs=(
            pl.BlockSpec((1, tall, wide), lambda i: (0, i, 0)),
            pl.BlockSpec((short, wide), lambda i: (i, 0)),
            pl.BlockSpec((short, wide), lambda i: (i, 0)),
        ),
        compiler_params=pltpu.CompilerParams(vmem_limit_bytes=48 * 1024 * 1024),
        name="outer_step",
    )(combined, left, right, params, momentum)
    return (new_error, new_params, new_momentum)


def solution(mesh):
    placed = (
        P("island", "fsdp", None),
        P("island", "fsdp", None),
        P(),
        P(("fsdp", "island"), None),
        P(("fsdp", "island"), None),
    )
    return jax.shard_map(
        functools.partial(shards, mesh.shape["island"], mesh.shape["fsdp"]),
        mesh=mesh,
        in_specs=placed,
        out_specs=(
            P("island", "fsdp", None),
            P(("fsdp", "island"), None),
            P(("fsdp", "island"), None),
        ),
        check_vma=False,
    )
```
